512 devices in a mesh: draw: 32 (over x_hi, z), img: 16 (over y, x_lo, core).
Axes of the slice: x: 4 (x_hi: 2, x_lo: 2; x = x_hi * 2 + x_lo), y: 4, z: 16, core: 2. Of those that a mesh axis runs over, the one named last changes fastest.
Arguments:
- features: bfloat16 [16, 32, 256, 1024], P('img', 'draw'), may hold values from -8 to 8
- cotangent: bfloat16 [16, 32, 256, 640], P('img', 'draw'), may hold values from -8 to 8
- time_index: int32 [16, 32], P('img', 'draw'), may hold values from 0 to 999, as said below
- mod_table: bfloat16 [1000, 1024], replicated, may hold values from -1.5 to 1.5
- weight: bfloat16 [1024, 640], replicated, may hold values from -0.1875 to 0.1875
Outputs:
- clipped_sum: float32 [1024, 640], P(('draw', 'img'))
- grad_input: bfloat16 [16, 32, 256, 1024], P('img', 'draw')
The draws below stay inside these ranges and needn't reach their ends.
Inputs may be any that keep to these rules, and one draw needn't show every extreme that they name: `time_index`: draw k's timestep lies in the k-th of 32 strata: from k * 1000 // 32 to k * 1000 // 32 + 1000 // 32 - 1, except that the last draw's stratum runs on to 999.
All inputs are finite; a program needn't handle non-finite values.
Results may differ from the reference program's by a relative error of at most 0.0075.
Values may be sent and summed in bfloat16 or wider, within the bound.
A program may use at most 64 MiB of HBM per device.

```python
import jax
import jax.numpy as jnp
from jax import lax

CIN = 1024
COUT = 640
PIX = 256
TSTEPS = 1000
DRAWS = 32
IMAGES = 16


def draw_features(key, part):
    key = jax.random.fold_in(key, 11)
    first_key, second_key, third_key, fourth_key = jax.random.split(key, 4)
    level = jax.random.uniform(third_key, (CIN,), jnp.float32, 0.0, 1.0)
    shared_part = jnp.sqrt(level)
    single_part = jnp.sqrt(1.0 - level)
    channel_scale = jnp.exp(jax.random.uniform(fourth_key, (CIN,), jnp.float32, -1.7, 1.7)) * 0.476
    shared = jax.random.normal(first_key, (IMAGES, 1, PIX, CIN), jnp.float32)
    single = jax.random.normal(second_key, (IMAGES, DRAWS, PIX, CIN), jnp.float32)
    values = (shared * shared_part + single * single_part) * channel_scale
    return jnp.clip(values, -8.0, 8.0).astype(jnp.bfloat16)


def draw_cotangent(key, part):
    key = jax.random.fold_in(key, 12)
    first_key, second_key, third_key, fourth_key, fifth_key = jax.random.split(key, 5)
    ramp = jnp.arange(IMAGES).astype(jnp.float32) / (IMAGES - 1) - 0.5
    scales = 10.0 ** ramp * jax.random.uniform(third_key, (IMAGES,), jnp.float32, 0.8, 1.25)
    sigma = 0.4 / jnp.sqrt(jnp.float32(PIX))
    level = jax.random.uniform(fifth_key, (COUT,), jnp.float32, 0.0, 1.0)
    shared_part = jnp.sqrt(level)
    single_part = jnp.sqrt(1.0 - level)
    shared = jax.random.normal(first_key, (IMAGES, 1, PIX, COUT), jnp.float32)
    single = jax.random.normal(second_key, (IMAGES, DRAWS, PIX, COUT), jnp.float32)
    columns = jnp.exp(jax.random.uniform(fourth_key, (COUT,), jnp.float32, -1.2, 1.2)) * 0.662
    values = (shared * shared_part + single * single_part) * sigma * scales[:, None, None, None] * columns
    return jnp.clip(values, -8.0, 8.0).astype(jnp.bfloat16)


def draw_time_index(key, part):
    key = jax.random.fold_in(key, 13)
    stride = TSTEPS // DRAWS
    starts = jnp.arange(DRAWS, dtype=jnp.int32) * TSTEPS // DRAWS
    jitter = jax.random.randint(key, (IMAGES, DRAWS), 0, stride, dtype=jnp.int32)
    values = starts[None, :] + jitter
    values = values.at[0, 0].set(0)
    values = values.at[0, DRAWS - 1].set(TSTEPS - 1)
    return values.astype(jnp.int32)


def bell_draw(rng, dims, spread, limit, held_as=jnp.bfloat16):
    result = jax.random.normal(rng, dims, jnp.float32) * spread
    return jnp.minimum(jnp.maximum(result, -limit), limit).astype(held_as)


def setup_inputs(seed: int = 0) -> dict:
    seeds = jax.random.split(jax.random.key(seed), 6)
    return {
        "features": draw_features(jax.random.fold_in(seeds[5], 71), 0),
        "cotangent": draw_cotangent(jax.random.fold_in(seeds[5], 71), 0),
        "time_index": draw_time_index(jax.random.fold_in(seeds[5], 71), 0),
        "mod_table": bell_draw(seeds[3], (TSTEPS, CIN), 0.3, 1.5),
        "weight": bell_draw(seeds[4], (CIN, COUT), CIN ** -0.5, 0.1875),
    }


def reference(features, cotangent, time_index, mod_table, weight):
    modulation = mod_table[time_index].astype(jnp.float32)
    gain = 1.0 + modulation[:, :, None, :]
    pre_act = features.astype(jnp.float32) * gain
    acts = jax.nn.silu(pre_act).astype(jnp.bfloat16)
    loss_scale = 1.0 + 2.0 * time_index.astype(jnp.float32) / (TSTEPS - 1)
    weighted = (cotangent.astype(jnp.float32) * loss_scale[:, :, None, None]).astype(jnp.bfloat16)
    back = jnp.dot(weighted.reshape(-1, COUT), weight.T, preferred_element_type=jnp.float32)
    back = back.reshape(features.shape)
    gate_sig = jax.nn.sigmoid(pre_act)
    grad_input = (back * gate_sig * (1.0 + pre_act * (1.0 - gate_sig)) * gain).astype(jnp.bfloat16)

    def image_grad(pair_in):
        acts_img, weighted_img = pair_in
        return jnp.dot(acts_img.reshape(-1, CIN).T, weighted_img.reshape(-1, COUT), preferred_element_type=jnp.float32) / DRAWS
    grads = lax.map(image_grad, (acts, weighted))
    norm_sq = lax.optimization_barrier(jnp.sum(grads * grads, axis=(1, 2)))
    clip_bound = 0.3 * jnp.sqrt(jnp.float32(CIN * COUT))
    clip = jnp.minimum(1.0, clip_bound / jnp.sqrt(norm_sq + 1e-06))
    clipped_sum = lax.optimization_barrier(jnp.sum(clip[:, None, None] * grads, axis=0))
    return (clipped_sum, grad_input)
```

```python
import functools
import math

import jax
import jax.numpy as jnp
from jax import lax
from jax.experimental import pallas as pl
from jax.experimental.pallas import tpu as pltpu
from jax.sharding import PartitionSpec as P

MESH = pl.DeviceIdType.MESH
F32 = jnp.float32
BF16 = jnp.bfloat16
LANES = 128


def sigmoid(v):
    return 1.0 / (1.0 + jnp.exp(-v))


def kernel(
    draws, images, table_rows, window,
    feat_hbm, cot_hbm, time_hbm, table_hbm, weight_hbm,
    sum_ref, gi_hbm,
    feat, cot, when, rows, weight, gain, weighted, grad, gi,
    send, recv, cross_out, cross_in, norm_out, norm_in, part_out, part_in,
    load_sem, store_sem, send_sem, recv_sem, cross_sem, norm_sem, norm_recv, part_sem, part_recv,
):
    pixels, in_width = feat.shape
    ring = draws // 2
    half_rows = in_width // 2
    piece = in_width // draws
    each = piece // images
    k = lax.axis_index("draw")
    image = lax.axis_index("img")
    high = lax.div(k, ring)
    z = lax.rem(k, ring)

    def at_z(offset):
        return high * ring + lax.rem(z + offset + ring, ring)

    first_row = lax.div(k * table_rows, draws)
    first_block = jnp.minimum(lax.div(first_row, 8), table_rows // 8 - window)
    loads = [
        pltpu.make_async_copy(time_hbm, when, load_sem.at[0]),
        pltpu.make_async_copy(table_hbm.at[pl.ds(first_block, window)], rows, load_sem.at[1]),
        pltpu.make_async_copy(cot_hbm.at[0, 0], cot, load_sem.at[2]),
        pltpu.make_async_copy(feat_hbm.at[0, 0], feat, load_sem.at[3]),
        pltpu.make_async_copy(weight_hbm, weight, load_sem.at[4]),
    ]
    for load in loads:
        load.start()

    barrier = pltpu.get_barrier_semaphore()

    def greet_draw(o, _):
        pl.semaphore_signal(
            barrier, inc=1, device_id={"draw": lax.rem(k + o, draws)}, device_id_type=MESH
        )
        return 0

    def greet_image(o, _):
        pl.semaphore_signal(
            barrier, inc=1, device_id={"img": lax.rem(image + o, images)}, device_id_type=MESH
        )
        return 0

    lax.fori_loop(1, draws, greet_draw, 0)
    lax.fori_loop(1, images, greet_image, 0)

    for load in loads[:3]:
        load.wait()
    step = when[...]
    index = (
        lax.broadcasted_iota(jnp.int32, (window, 8, 1), 0) * 8
        + lax.broadcasted_iota(jnp.int32, (window, 8, 1), 1)
        + first_block * 8
    )
    chosen = jnp.where(index == step.reshape(1, 1, 1), rows[...].astype(F32), 0.0)
    gain[...] = 1.0 + jnp.sum(jnp.sum(chosen, axis=0), axis=0, keepdims=True)
    loss_scale = 1.0 + 2.0 * step.astype(F32) / (table_rows - 1)
    weighted[...] = (cot[...].astype(F32) * loss_scale).astype(BF16)
    loads[3].wait()

    for block in range(in_width // LANES):
        at = pl.ds(block * LANES, LANES)
        pre_act = feat[:, at].astype(F32) * gain[:, at]
        acts = (pre_act * sigmoid(pre_act)).astype(BF16)
        grad[at, :] = lax.dot_general(
            acts, weighted[...], (((0,), (0,)), ((), ())), preferred_element_type=F32
        )

    pl.semaphore_wait(barrier, draws - 1 + images - 1)

    streams = []
    for half in range(2):
        for way in range(2):
            hops = ring // 2 if half == way else ring // 2 - 1
            streams.append((half, way, hops))

    def ring_copy(half, way, left):
        return pltpu.make_async_remote_copy(
            src_ref=send.at[half, way, left],
            dst_ref=recv.at[half, way, left],
            send_sem=send_sem.at[half, way, left],
            recv_sem=recv_sem.at[half, way, left],
            device_id={"draw": at_z(1 if way == 0 else -1)},
            device_id_type=MESH,
        )

    def own(half, offset):
        start = half * half_rows + lax.rem(z + offset + ring, ring) * piece
        return grad[pl.ds(pl.multiple_of(start, piece), piece), :]

    def grad_input_block(block):
        at = pl.ds(block * LANES, LANES)
        back = lax.dot_general(
            weighted[...], weight[at, :], (((1,), (1,)), ((), ())), preferred_element_type=F32
        )
        scale = gain[:, at]
        pre_act = feat[:, at].astype(F32) * scale
        gate = sigmoid(pre_act)
        gi[:, at] = (back * gate * (1.0 + pre_act * (1.0 - gate)) * scale).astype(BF16)

    blocks = in_width // LANES
    steps = ring // 2
    done = 0
    for j in range(steps):
        for half, way, hops in streams:
            if j >= hops:
                continue
            left = hops - 1 - j
            term = own(half, (hops - j) if way == 0 else -(hops - j))
            if j > 0:
                ring_copy(half, way, left + 1).wait_recv()
                term = term + recv[half, way, left + 1].astype(F32)
            send[half, way, left] = term.astype(BF16)
            ring_copy(half, way, left).start()
        if j == 0:
            loads[4].wait()
        target = blocks * (j + 1) // steps
        while done < target:
            grad_input_block(done)
            done += 1
    store = pltpu.make_async_copy(gi, gi_hbm.at[0, 0], store_sem)
    store.start()

    for half in range(2):
        for way in range(2):
            ring_copy(half, way, 0).wait_recv()

    def whole(half):
        return own(half, 0) + recv[half, 0, 0].astype(F32) + recv[half, 1, 0].astype(F32)

    cross_out[...] = whole(1 - high).astype(BF16)
    cross = pltpu.make_async_remote_copy(
        src_ref=cross_out,
        dst_ref=cross_in,
        send_sem=cross_sem.at[0],
        recv_sem=cross_sem.at[1],
        device_id={"draw": (1 - high) * ring + z},
        device_id_type=MESH,
    )
    cross.start()
    mine = whole(high)
    cross.wait_recv()
    mine = (mine + cross_in[...].astype(F32)) * (1.0 / draws)

    square = mine * mine
    tile = square[:, 0:LANES]
    for c in range(1, square.shape[1] // LANES):
        tile = tile + square[:, c * LANES : (c + 1) * LANES]
    tile = jnp.sum(tile.reshape(piece // 8, 8, LANES), axis=0)
    norm_out[...] = tile

    def norm_copy(o):
        return pltpu.make_async_remote_copy(
            src_ref=norm_out,
            dst_ref=norm_in.at[o - 1],
            send_sem=norm_sem.at[o - 1],
            recv_sem=norm_recv.at[o - 1],
            device_id={"draw": lax.rem(k + o, draws)},
            device_id_type=MESH,
        )

    def norm_start(o, _):
        norm_copy(o).start()
        return 0

    def norm_wait(o, _):
        norm_copy(o).wait_recv()
        return 0

    lax.fori_loop(1, draws, norm_start, 0)
    lax.fori_loop(1, draws, norm_wait, 0)
    total = jnp.sum(norm_in[...], axis=0) + tile
    norm_sq = jnp.sum(jnp.sum(total, axis=0, keepdims=True), axis=1, keepdims=True)
    bound = 0.3 * math.sqrt(in_width * cot.shape[1])
    clip = jnp.minimum(1.0, bound / jnp.sqrt(norm_sq + 1e-06))
    mine = mine * clip

    for j in range(images):
        part_out[j] = mine[j * each : (j + 1) * each, :]

    def part_copy(o):
        to = lax.rem(image + o, images)
        return pltpu.make_async_remote_copy(
            src_ref=part_out.at[to],
            dst_ref=part_in.at[o],
            send_sem=part_sem.at[o],
            recv_sem=part_recv.at[o],
            device_id={"img": to},
            device_id_type=MESH,
        )

    def part_start(o, _):
        part_copy(o).start()
        return 0

    def part_wait(o, _):
        part_copy(o).wait_recv()
        return 0

    lax.fori_loop(1, images, part_start, 0)
    part_in[0] = part_out[image]
    lax.fori_loop(1, images, part_wait, 0)
    sum_ref[...] = jnp.sum(part_in[...], axis=0)

    def norm_sent(o, _):
        norm_copy(o).wait_send()
        return 0

    def part_sent(o, _):
        part_copy(o).wait_send()
        return 0

    for half, way, hops in streams:
        for left in range(hops):
            ring_copy(half, way, left).wait_send()
    cross.wait_send()
    lax.fori_loop(1, draws, norm_sent, 0)
    lax.fori_loop(1, images, part_sent, 0)
    store.wait()


def local(draws, images, features, cotangent, time_index, mod_table, weight):
    pixels, in_width = features.shape[2:]
    out_width = cotangent.shape[3]
    table_rows = mod_table.shape[0]
    stratum = table_rows - (draws - 1) * table_rows // draws
    window = (stratum + 14) // 8
    piece = in_width // draws
    each = piece // images
    hops = draws // 4
    dma = pltpu.SemaphoreType.DMA
    return pl.pallas_call(
        functools.partial(kernel, draws, images, table_rows, window),
        out_shape=(
            jax.ShapeDtypeStruct((each, out_width), F32),
            jax.ShapeDtypeStruct(features.shape, BF16),
        ),
        in_specs=[pl.BlockSpec(memory_space=pl.ANY)] * 5,
        out_specs=(
            pl.BlockSpec(memory_space=pltpu.VMEM),
            pl.BlockSpec(memory_space=pl.ANY),
        ),
        scratch_shapes=[
            pltpu.VMEM((pixels, in_width), BF16),
            pltpu.VMEM((pixels, out_width), BF16),
            pltpu.VMEM((1, 1), jnp.int32),
            pltpu.VMEM((window, 8, in_width), BF16),
            pltpu.VMEM((in_width, out_width), BF16),
            pltpu.VMEM((1, in_width), F32),
            pltpu.VMEM((pixels, out_width), BF16),
            pltpu.VMEM((in_width, out_width), F32),
            pltpu.VMEM((pixels, in_width), BF16),
            pltpu.VMEM((2, 2, hops, piece, out_width), BF16),
            pltpu.VMEM((2, 2, hops, piece, out_width), BF16),
            pltpu.VMEM((piece, out_width), BF16),
            pltpu.VMEM((piece, out_width), BF16),
            pltpu.VMEM((8, LANES), F32),
            pltpu.VMEM((draws - 1, 8, LANES), F32),
            pltpu.VMEM((images, each, out_width), F32),
            pltpu.VMEM((images, each, out_width), F32),
            dma((5,)),
            dma,
            dma((2, 2, hops)),
            dma((2, 2, hops)),
            dma((2,)),
            dma((draws - 1,)),
            dma((draws - 1,)),
            dma((images,)),
            dma((images,)),
        ],
        compiler_params=pltpu.CompilerParams(
            collective_id=0, has_side_effects=True, vmem_limit_bytes=48 * 2**20
        ),
        cost_estimate=pl.CostEstimate(
            flops=4 * pixels * in_width * out_width,
            bytes_accessed=2 * (2 * pixels * in_width + pixels * out_width + in_width * out_width),
            transcendentals=2 * pixels * in_width,
        ),
    )(
        features,
        cotangent,
        time_index,
        mod_table.reshape(table_rows // 8, 8, in_width),
        weight,
    )


def solution(mesh):
    in_specs = (
        P("img", "draw", None, None),
        P("img", "draw", None, None),
        P("img", "draw"),
        P(),
        P(),
    )
    out_specs = (P(("draw", "img"), None), P("img", "draw", None, None))
    body = functools.partial(local, mesh.shape["draw"], mesh.shape["img"])
    return jax.shard_map(body, mesh=mesh, in_specs=in_specs, out_specs=out_specs, check_vma=False)
```

```python
import functools
import math

import jax
import jax.numpy as jnp
from jax import lax
from jax.experimental import pallas as pl
from jax.experimental.pallas import tpu as pltpu
from jax.sharding import PartitionSpec as P

MESH = pl.DeviceIdType.MESH
F32 = jnp.float32
BF16 = jnp.bfloat16
LANES = 128
CROSS_FIRST = 512
LAG = 1
PART = BF16
TREES = {
    8: {8: 7, 7: 6, 6: 5, 5: 0, 4: 3, 3: 2, 2: 1, 1: 0},
    7: {7: 6, 6: 5, 5: 0, 4: 3, 3: 2, 2: 1, 1: 0},
}


def sigmoid(v):
    return 1.0 / (1.0 + jnp.exp(-v))


def tree_levels(tree):
    level = {}
    for node in sorted(tree, reverse=True):
        level[node] = max([level[c] + 1 for c in tree if tree[c] == node], default=0)
    return level


def kernel(
    draws, images, table_rows, window,
    feat_hbm, cot_hbm, time_hbm, table_hbm, weight_hbm,
    sum_ref, gi_hbm,
    feat, cot, when, rows, weight, gain, weighted, grad, gi,
    first_out, first_in, xsend, xrecv, zsend, zrecv, cross_out, cross_in,
    norm_out, norm_in, part_out, part_in,
    load_sem, store_sem, first_send, first_recv, xsend_sem, xrecv_sem, zsend_sem, zrecv_sem,
    cross_sem, norm_sem, part_sem,
):
    in_width = feat.shape[1]
    out_width = cot.shape[1]
    ring = draws // 2
    half_rows = in_width // 2
    piece = in_width // draws
    each = piece // images
    first_cols = slice(0, CROSS_FIRST)
    late_cols = slice(CROSS_FIRST, out_width)
    k = lax.axis_index("draw")
    image = lax.axis_index("img")
    high = lax.div(k, ring)
    z = lax.rem(k, ring)

    def around(offset):
        return lax.rem(z + (offset + ring), ring)

    def at_z(offset):
        return {"draw": high * ring + around(offset)}

    partner = {"draw": (1 - high) * ring + z}

    first_row = lax.div(k * table_rows, draws)
    first_block = jnp.minimum(lax.div(first_row, 8), table_rows // 8 - window)
    loads = [
        pltpu.make_async_copy(time_hbm, when, load_sem.at[0]),
        pltpu.make_async_copy(table_hbm.at[pl.ds(first_block, window)], rows, load_sem.at[1]),
        pltpu.make_async_copy(cot_hbm.at[0, 0], cot, load_sem.at[2]),
        pltpu.make_async_copy(feat_hbm.at[0, 0], feat, load_sem.at[3]),
        pltpu.make_async_copy(weight_hbm, weight, load_sem.at[4]),
    ]
    for load in loads:
        load.start()

    trees = {ring // 2: TREES[ring // 2], ring // 2 - 1: TREES[ring // 2 - 1]}
    reach = sorted({node - tree[node] for tree in trees.values() for node in tree})
    barrier = pltpu.get_barrier_semaphore()
    for hop in reach:
        for offset in (hop, -hop):
            pl.semaphore_signal(barrier, inc=1, device_id=at_z(offset), device_id_type=MESH)
    pl.semaphore_signal(barrier, inc=1, device_id=partner, device_id_type=MESH)

    def greet_image(o, _):
        pl.semaphore_signal(
            barrier, inc=1, device_id={"img": lax.rem(image + o, images)}, device_id_type=MESH
        )
        return 0

    lax.fori_loop(1, images, greet_image, 0)

    for load in loads[:3]:
        load.wait()
    step = when[...]
    index = (
        lax.broadcasted_iota(jnp.int32, (window, 8, 1), 0) * 8
        + lax.broadcasted_iota(jnp.int32, (window, 8, 1), 1)
        + first_block * 8
    )
    chosen = jnp.where(index == step.reshape(1, 1, 1), rows[...].astype(F32), 0.0)
    gain[...] = 1.0 + jnp.sum(jnp.sum(chosen, axis=0), axis=0, keepdims=True)
    loss_scale = 1.0 + 2.0 * step.astype(F32) / (table_rows - 1)
    weighted[...] = (cot[...].astype(F32) * loss_scale).astype(BF16)
    loads[3].wait()

    for block in range(in_width // LANES):
        at = pl.ds(block * LANES, LANES)
        pre_act = feat[:, at].astype(F32) * gain[:, at]
        acts = (pre_act * sigmoid(pre_act)).astype(BF16)
        grad[at, :] = lax.dot_general(
            acts, weighted[...], (((0,), (0,)), ((), ())), preferred_element_type=F32
        )

    pl.semaphore_wait(barrier, 2 * len(reach) + images)

    def own(half, offset, cols):
        start = half * half_rows + around(offset) * piece
        return grad[pl.ds(pl.multiple_of(start, piece), piece), cols]

    def first_copy(n):
        return pltpu.make_async_remote_copy(
            src_ref=first_out.at[n],
            dst_ref=first_in.at[n],
            send_sem=first_send.at[n],
            recv_sem=first_recv.at[n],
            device_id=partner,
            device_id_type=MESH,
        )

    def first_start(n):
        first_out[n] = own(1 - high, n, first_cols).astype(BF16)
        first_copy(n).start()

    arrived = set()

    def first_own(offset):
        n = offset % ring
        if n not in arrived:
            arrived.add(n)
            first_copy(n).wait_recv()
        return own(high, offset, first_cols) + first_in[n].astype(F32)

    def zcopy(half, way, node, hop):
        return pltpu.make_async_remote_copy(
            src_ref=zsend.at[half, way, node - 1],
            dst_ref=zrecv.at[half, way, node - 1],
            send_sem=zsend_sem.at[half, way, node - 1],
            recv_sem=zrecv_sem.at[half, way, node - 1],
            device_id=at_z(hop if way == 0 else -hop),
            device_id_type=MESH,
        )

    def xcopy(way, node, hop):
        return pltpu.make_async_remote_copy(
            src_ref=xsend.at[way, node - 1],
            dst_ref=xrecv.at[way, node - 1],
            send_sem=xsend_sem.at[way, node - 1],
            recv_sem=xrecv_sem.at[way, node - 1],
            device_id=at_z(hop if way == 0 else -hop),
            device_id_type=MESH,
        )

    jobs = []
    for way in range(2):
        for half in range(2):
            tree = trees[ring // 2 if half == way else ring // 2 - 1]
            for node, level in tree_levels(tree).items():
                jobs.append((level, 0, -node, half, way, tree))
        tree = trees[ring // 2 if way == 0 else ring // 2 - 1]
        for node, level in tree_levels(tree).items() if CROSS_FIRST else ():
            jobs.append((level + LAG, 1, -node, 0, way, tree))
    jobs.sort(key=lambda job: job[:5])

    def children(tree, node):
        return [c for c in tree if tree[c] == node]

    def total(kind, half, way, tree, node, offset):
        if kind == 0:
            term = own(half, offset, late_cols)
            for c in children(tree, node):
                zcopy(half, way, c, c - node).wait_recv()
                term = term + zrecv[half, way, c - 1].astype(F32)
        else:
            term = first_own(offset)
            for c in children(tree, node):
                xcopy(way, c, c - node).wait_recv()
                term = term + xrecv[way, c - 1].astype(F32)
        return term

    def grad_input_block(block):
        at = pl.ds(block * LANES, LANES)
        back = lax.dot_general(
            weighted[...], weight[at, :], (((1,), (1,)), ((), ())), preferred_element_type=F32
        )
        scale = gain[:, at]
        pre_act = feat[:, at].astype(F32) * scale
        gate = sigmoid(pre_act)
        gi[:, at] = (back * gate * (1.0 + pre_act * (1.0 - gate)) * scale).astype(BF16)

    if CROSS_FIRST:
        order = []
        for level, kind, minus, half, way, tree in jobs:
            if kind == 1:
                n = (-minus if way == 0 else minus) % ring
                if n not in order:
                    order.append(n)
        order.append(0)
        for n in order:
            first_start(n)
    blocks = in_width // LANES
    done = 0
    sent = []
    last = jobs[-1][0]
    for at, (level, kind, minus, half, way, tree) in enumerate(jobs):
        node = -minus
        offset = node if way == 0 else -node
        hop = node - tree[node]
        term = total(kind, half, way, tree, node, offset).astype(BF16)
        if kind == 0:
            zsend[half, way, node - 1] = term
            copy = zcopy(half, way, node, hop)
        else:
            xsend[way, node - 1] = term
            copy = xcopy(way, node, hop)
        copy.start()
        sent.append(copy)
        if at + 1 == len(jobs) or jobs[at + 1][0] > level:
            target = blocks * (level + 1) // (last + 1)
            if done == 0 and target > 0:
                loads[4].wait()
            while done < target:
                grad_input_block(done)
                done += 1
    store = pltpu.make_async_copy(gi, gi_hbm.at[0, 0], store_sem)
    store.start()

    root8 = set(children(trees[ring // 2], 0))
    root7 = set(children(trees[ring // 2 - 1], 0))
    for half in range(2):
        for way in range(2):
            for c in sorted(root8 if half == way else root7, reverse=True):
                zcopy(half, way, c, c).wait_recv()
    shared = sorted(root8 & root7)

    def whole(half):
        value = own(half, 0, late_cols)
        for way in range(2):
            for c in shared:
                value = value + zrecv[half, way, c - 1].astype(F32)
        for c in sorted(root8 - root7):
            value = value + zrecv[half, half, c - 1].astype(F32)
        for c in sorted(root7 - root8):
            value = value + zrecv[half, 1 - half, c - 1].astype(F32)
        return value

    cross_out[...] = whole(1 - high).astype(BF16)
    cross = pltpu.make_async_remote_copy(
        src_ref=cross_out,
        dst_ref=cross_in,
        send_sem=cross_sem.at[0],
        recv_sem=cross_sem.at[1],
        device_id=partner,
        device_id_type=MESH,
    )
    cross.start()
    sent.append(cross)
    parts = []
    if CROSS_FIRST:
        value = first_own(0)
        for way in range(2):
            tree = trees[ring // 2 if way == 0 else ring // 2 - 1]
            for c in children(tree, 0):
                xcopy(way, c, c).wait_recv()
                value = value + xrecv[way, c - 1].astype(F32)
        parts.append(value)
        sent += [first_copy(n) for n in order]
    value = whole(high)
    cross.wait_recv()
    parts.append(value + cross_in[...].astype(F32))
    mine = jnp.concatenate(parts, axis=1) * (1.0 / draws)

    def finish():
        for copy in sent:
            copy.wait_send()
        store.wait()


    square = mine * mine
    tile = square[:, 0:LANES]
    for c in range(1, out_width // LANES):
        tile = tile + square[:, c * LANES : (c + 1) * LANES]
    norm_out[...] = jnp.sum(tile, axis=0, keepdims=True)

    def norm_start(o, _):
        pltpu.make_async_remote_copy(
            src_ref=norm_out,
            dst_ref=norm_in.at[o],
            send_sem=norm_sem.at[0],
            recv_sem=norm_sem.at[1],
            device_id={"draw": lax.rem(k + o, draws)},
            device_id_type=MESH,
        ).start()
        return 0

    lax.fori_loop(1, draws, norm_start, 0)
    norm_in[0] = norm_out[...]
    norm_all = norm_in.at[pl.ds(1, draws - 1)]
    pltpu.make_async_copy(norm_all, norm_all, norm_sem.at[1]).wait()
    norm_sq = jnp.sum(jnp.sum(norm_in[...], axis=0), axis=1, keepdims=True)
    bound = 0.3 * math.sqrt(in_width * out_width)
    clip = jnp.minimum(1.0, bound / jnp.sqrt(norm_sq + 1e-06))
    mine = mine * clip

    for j in range(images):
        part_out[j] = mine[j * each : (j + 1) * each, :].astype(part_out.dtype)

    def part_start(o, _):
        to = lax.rem(image + o, images)
        pltpu.make_async_remote_copy(
            src_ref=part_out.at[to],
            dst_ref=part_in.at[o],
            send_sem=part_sem.at[0],
            recv_sem=part_sem.at[1],
            device_id={"img": to},
            device_id_type=MESH,
        ).start()
        return 0

    lax.fori_loop(1, images, part_start, 0)
    part_in[0] = part_out[image]
    part_all = part_in.at[pl.ds(1, images - 1)]
    pltpu.make_async_copy(part_all, part_all, part_sem.at[1]).wait()
    sum_ref[...] = jnp.sum(part_in[...].astype(F32), axis=0)

    finish()
    pltpu.make_async_copy(norm_all, norm_all, norm_sem.at[0]).wait()
    pltpu.make_async_copy(part_all, part_all, part_sem.at[0]).wait()


def local(draws, images, features, cotangent, time_index, mod_table, weight):
    pixels, in_width = features.shape[2:]
    out_width = cotangent.shape[3]
    table_rows = mod_table.shape[0]
    stratum = table_rows - (draws - 1) * table_rows // draws
    window = (stratum + 14) // 8
    piece = in_width // draws
    each = piece // images
    hops = draws // 4
    first = CROSS_FIRST or LANES
    late = out_width - CROSS_FIRST
    dma = pltpu.SemaphoreType.DMA
    return pl.pallas_call(
        functools.partial(kernel, draws, images, table_rows, window),
        out_shape=(
            jax.ShapeDtypeStruct((each, out_width), F32),
            jax.ShapeDtypeStruct(features.shape, BF16),
        ),
        in_specs=[pl.BlockSpec(memory_space=pltpu.HBM)] * 5,
        out_specs=(
            pl.BlockSpec(memory_space=pltpu.VMEM),
            pl.BlockSpec(memory_space=pl.ANY),
        ),
        scratch_shapes=[
            pltpu.VMEM((pixels, in_width), BF16),
            pltpu.VMEM((pixels, out_width), BF16),
            pltpu.VMEM((1, 1), jnp.int32),
            pltpu.VMEM((window, 8, in_width), BF16),
            pltpu.VMEM((in_width, out_width), BF16),
            pltpu.VMEM((1, in_width), F32),
            pltpu.VMEM((pixels, out_width), BF16),
            pltpu.VMEM((in_width, out_width), F32),
            pltpu.VMEM((pixels, in_width), BF16),
            pltpu.VMEM((draws // 2, piece, first), BF16),
            pltpu.VMEM((draws // 2, piece, first), BF16),
            pltpu.VMEM((2, hops, piece, first), BF16),
            pltpu.VMEM((2, hops, piece, first), BF16),
            pltpu.VMEM((2, 2, hops, piece, late), BF16),
            pltpu.VMEM((2, 2, hops, piece, late), BF16),
            pltpu.VMEM((piece, late), BF16),
            pltpu.VMEM((piece, late), BF16),
            pltpu.VMEM((1, LANES), F32),
            pltpu.VMEM((draws, 1, LANES), F32),
            pltpu.VMEM((images, each, out_width), PART),
            pltpu.VMEM((images, each, out_width), PART),
            dma((5,)),
            dma,
            dma((draws // 2,)),
            dma((draws // 2,)),
            dma((2, hops)),
            dma((2, hops)),
            dma((2, 2, hops)),
            dma((2, 2, hops)),
            dma((2,)),
            dma((2,)),
            dma((2,)),
        ],
        compiler_params=pltpu.CompilerParams(
            collective_id=0, has_side_effects=True, vmem_limit_bytes=60 * 2**20
        ),
        cost_estimate=pl.CostEstimate(
            flops=4 * pixels * in_width * out_width,
            bytes_accessed=2 * (2 * pixels * in_width + pixels * out_width + in_width * out_width),
            transcendentals=2 * pixels * in_width,
        ),
    )(
        features,
        cotangent,
        time_index,
        mod_table.reshape(table_rows // 8, 8, in_width),
        weight,
    )


def solution(mesh):
    in_specs = (
        P("img", "draw", None, None),
        P("img", "draw", None, None),
        P("img", "draw"),
        P(),
        P(),
    )
    out_specs = (P(("draw", "img"), None), P("img", "draw", None, None))
    body = functools.partial(local, mesh.shape["draw"], mesh.shape["img"])
    return jax.shard_map(body, mesh=mesh, in_specs=in_specs, out_specs=out_specs, check_vma=False)
```

```python
import functools
import math

import jax
import jax.numpy as jnp
from jax import lax
from jax.experimental import pallas as pl
from jax.experimental.pallas import tpu as pltpu
from jax.sharding import PartitionSpec as P

MESH = pl.DeviceIdType.MESH
F32 = jnp.float32
BF16 = jnp.bfloat16
LANES = 128
LAG = 0
NEAR = {3: 2, 2: 1, 1: 0}
FAR = {8: 6, 7: 6, 6: 4, 5: 4, 4: 0}


def sigmoid(v):
    return 1.0 / (1.0 + jnp.exp(-v))


def tree_levels(tree):
    level = {}
    for node in sorted(tree, reverse=True):
        level[node] = max([level[c] + 1 for c in tree if tree[c] == node], default=0)
    return level


def kernel(
    draws, images, table_rows, window,
    feat_hbm, cot_hbm, time_hbm, table_hbm, weight_hbm,
    sum_ref, gi_ref,
    feat, cot, when, rows, weight, gain, weighted, grad,
    first_out, first_in, xsend, xrecv, zsend, zrecv, both, cross_out, cross_in,
    plane_out, plane_in, norm_out, norm_in, part_out, part_in,
    load_sem, first_send, first_recv, xsend_sem, xrecv_sem, zsend_sem, zrecv_sem,
    cross_sem, plane_sem, norm_sem, part_sem,
):
    in_width = feat.shape[1]
    out_width = cot.shape[1]
    ring = draws // 2
    half_rows = in_width // 2
    piece = in_width // draws
    each = piece // images
    k = lax.axis_index("draw")
    image = lax.axis_index("img")
    high = lax.div(k, ring)
    z = lax.rem(k, ring)

    def around(offset):
        return lax.rem(z + (offset + ring), ring)

    def at_z(offset):
        return {"draw": high * ring + around(offset)}

    partner = {"draw": (1 - high) * ring + z}

    first_row = lax.div(k * table_rows, draws)
    first_block = jnp.minimum(lax.div(first_row, 8), table_rows // 8 - window)
    loads = [
        pltpu.make_async_copy(time_hbm, when, load_sem.at[0]),
        pltpu.make_async_copy(table_hbm.at[pl.ds(first_block, window)], rows, load_sem.at[1]),
        pltpu.make_async_copy(cot_hbm.at[0, 0], cot, load_sem.at[2]),
        pltpu.make_async_copy(feat_hbm.at[0, 0], feat, load_sem.at[3]),
        pltpu.make_async_copy(weight_hbm, weight, load_sem.at[4]),
    ]
    for load in loads:
        load.start()

    near, far = (NEAR, NEAR), (FAR, {c: p for c, p in FAR.items() if c != ring // 2})
    reach = sorted({c - p for tree in (NEAR, FAR) for c, p in tree.items()})
    barrier = pltpu.get_barrier_semaphore()
    for hop in reach:
        for offset in (hop, -hop):
            pl.semaphore_signal(barrier, inc=1, device_id=at_z(offset), device_id_type=MESH)
    pl.semaphore_signal(barrier, inc=1, device_id=partner, device_id_type=MESH)

    def greet_image(o, _):
        pl.semaphore_signal(
            barrier, inc=1, device_id={"img": lax.rem(image + o, images)}, device_id_type=MESH
        )
        return 0

    lax.fori_loop(1, images, greet_image, 0)

    for load in loads[:3]:
        load.wait()
    step = when[...]
    index = (
        lax.broadcasted_iota(jnp.int32, (window, 8, 1), 0) * 8
        + lax.broadcasted_iota(jnp.int32, (window, 8, 1), 1)
        + first_block * 8
    )
    chosen = jnp.where(index == step.reshape(1, 1, 1), rows[...].astype(F32), 0.0)
    gain[...] = 1.0 + jnp.sum(jnp.sum(chosen, axis=0), axis=0, keepdims=True)
    loss_scale = 1.0 + 2.0 * step.astype(F32) / (table_rows - 1)
    weighted[...] = (cot[...].astype(F32) * loss_scale).astype(BF16)
    loads[3].wait()

    for block in range(in_width // LANES):
        at = pl.ds(block * LANES, LANES)
        pre_act = feat[:, at].astype(F32) * gain[:, at]
        acts = (pre_act * sigmoid(pre_act)).astype(BF16)
        grad[at, :] = lax.dot_general(
            acts, weighted[...], (((0,), (0,)), ((), ())), preferred_element_type=F32
        )

    pl.semaphore_wait(barrier, 2 * len(reach) + images)

    def own(half, offset):
        start = half * half_rows + around(offset) * piece
        return grad[pl.ds(pl.multiple_of(start, piece), piece), :]

    def first_copy(n):
        return pltpu.make_async_remote_copy(
            src_ref=first_out.at[n],
            dst_ref=first_in.at[n],
            send_sem=first_send.at[n],
            recv_sem=first_recv.at[n],
            device_id=partner,
            device_id_type=MESH,
        )

    def near_copy(half, way, node, hop):
        return pltpu.make_async_remote_copy(
            src_ref=zsend.at[half, way, node - 1],
            dst_ref=zrecv.at[half, way, node - 1],
            send_sem=zsend_sem.at[half, way, node - 1],
            recv_sem=zrecv_sem.at[half, way, node - 1],
            device_id=at_z(hop if way == 0 else -hop),
            device_id_type=MESH,
        )

    def far_copy(way, node, hop):
        return pltpu.make_async_remote_copy(
            src_ref=xsend.at[way, node - 1],
            dst_ref=xrecv.at[way, node - 1],
            send_sem=xsend_sem.at[way, node - 1],
            recv_sem=xrecv_sem.at[way, node - 1],
            device_id=at_z(hop if way == 0 else -hop),
            device_id_type=MESH,
        )

    def children(tree, node):
        return [c for c in tree if tree[c] == node]

    def near_sum(half, way, node, term):
        for c in children(near[way], node):
            near_copy(half, way, c, c - node).wait_recv()
            term = term + zrecv[half, way, c - 1].astype(F32)
        return term

    def far_sum(way, node, term):
        for c in children(far[way], node):
            far_copy(way, c, c - node).wait_recv()
            term = term + xrecv[way, c - 1].astype(F32)
        return term

    def grad_input_block(block):
        at = pl.ds(block * LANES, LANES)
        back = lax.dot_general(
            weighted[...], weight[at, :], (((1,), (1,)), ((), ())), preferred_element_type=F32
        )
        scale = gain[:, at]
        pre_act = feat[:, at].astype(F32) * scale
        gate = sigmoid(pre_act)
        gi_ref[0, 0, :, at] = (back * gate * (1.0 + pre_act * (1.0 - gate)) * scale).astype(BF16)

    jobs = []
    for way in range(2):
        for node, level in tree_levels(near[way]).items():
            jobs += [(level, 0, -node, half, way) for half in range(2)]
        for node, level in tree_levels(far[way]).items():
            jobs.append((level + LAG, 1, -node, 0, way))
    jobs.sort()
    sent = []
    for _, kind, minus, _, way in jobs:
        if kind == 1:
            offset = -minus if way == 0 else minus
            first_out[offset % ring] = own(1 - high, offset).astype(BF16)
            sent.append(first_copy(offset % ring))
            sent[-1].start()
    blocks = in_width // LANES
    done = 0
    last = jobs[-1][0]
    for at, (level, kind, minus, half, way) in enumerate(jobs):
        node = -minus
        offset = node if way == 0 else -node
        if kind == 0:
            term = near_sum(half, way, node, own(half, offset))
            zsend[half, way, node - 1] = term.astype(BF16)
            copy = near_copy(half, way, node, node - near[way][node])
        else:
            first_copy(offset % ring).wait_recv()
            term = own(high, offset) + first_in[offset % ring].astype(F32)
            xsend[way, node - 1] = far_sum(way, node, term).astype(BF16)
            copy = far_copy(way, node, node - far[way][node])
        copy.start()
        sent.append(copy)
        if at + 1 == len(jobs) or jobs[at + 1][0] > level:
            target = blocks * (level + 1) // (last + 1)
            if done == 0 and target > 0:
                loads[4].wait()
            while done < target:
                grad_input_block(done)
                done += 1

    for half in range(2):
        term = own(half, 0)
        for way in range(2):
            term = near_sum(half, way, 0, term)
        both[half] = term
    cross_out[...] = both[1 - high].astype(BF16)
    cross = pltpu.make_async_remote_copy(
        src_ref=cross_out,
        dst_ref=cross_in,
        send_sem=cross_sem.at[0],
        recv_sem=cross_sem.at[1],
        device_id=partner,
        device_id_type=MESH,
    )
    cross.start()
    sent.append(cross)
    mine = both[high]
    cross.wait_recv()
    mine = mine + cross_in[...].astype(F32)
    for way in range(2):
        mine = far_sum(way, 0, mine)
    mine = mine * (1.0 / draws)

    def finish():
        for copy in sent:
            copy.wait_send()


    square = mine * mine
    tile = square[:, 0:LANES]
    for c in range(1, out_width // LANES):
        tile = tile + square[:, c * LANES : (c + 1) * LANES]
    plane_out[...] = jnp.sum(tile, axis=0, keepdims=True)

    def plane_start(o, _):
        pltpu.make_async_remote_copy(
            src_ref=plane_out,
            dst_ref=plane_in.at[o],
            send_sem=plane_sem.at[0],
            recv_sem=plane_sem.at[1],
            device_id={"img": lax.rem(image + o, images)},
            device_id_type=MESH,
        ).start()
        return 0

    lax.fori_loop(1, images, plane_start, 0)
    for j in range(images):
        part_out[j] = mine[j * each : (j + 1) * each, :].astype(BF16)

    def part_start(o, _):
        to = lax.rem(image + o, images)
        pltpu.make_async_remote_copy(
            src_ref=part_out.at[to],
            dst_ref=part_in.at[o],
            send_sem=part_sem.at[0],
            recv_sem=part_sem.at[1],
            device_id={"img": to},
            device_id_type=MESH,
        ).start()
        return 0

    lax.fori_loop(1, images, part_start, 0)
    plane_in[0] = plane_out[...]
    part_in[0] = part_out[image]
    plane_all = plane_in.at[pl.ds(1, images - 1)]
    pltpu.make_async_copy(plane_all, plane_all, plane_sem.at[1]).wait()

    lane = lax.broadcasted_iota(jnp.int32, (images, 1, LANES), 2)
    slot = lax.broadcasted_iota(jnp.int32, (images, 1, LANES), 0)
    shares = jnp.sum(plane_in[...], axis=2, keepdims=True)
    norm_out[...] = jnp.sum(jnp.where(lane == slot, shares, 0.0), axis=0)

    def norm_start(o, _):
        pltpu.make_async_remote_copy(
            src_ref=norm_out,
            dst_ref=norm_in.at[o],
            send_sem=norm_sem.at[0],
            recv_sem=norm_sem.at[1],
            device_id={"draw": lax.rem(k + o, draws)},
            device_id_type=MESH,
        ).start()
        return 0

    lax.fori_loop(1, draws, norm_start, 0)
    norm_in[0] = norm_out[...]
    part_all = part_in.at[pl.ds(1, images - 1)]
    pltpu.make_async_copy(part_all, part_all, part_sem.at[1]).wait()
    finish()
    pltpu.make_async_copy(plane_all, plane_all, plane_sem.at[0]).wait()
    pltpu.make_async_copy(part_all, part_all, part_sem.at[0]).wait()
    norm_all = norm_in.at[pl.ds(1, draws - 1)]
    pltpu.make_async_copy(norm_all, norm_all, norm_sem.at[1]).wait()
    norm_sq = jnp.sum(norm_in[...], axis=0)
    bound = 0.3 * math.sqrt(in_width * out_width)
    clip = jnp.minimum(1.0, bound / jnp.sqrt(norm_sq + 1e-06))
    total = part_in[0].astype(F32) * clip[:, 0:1]
    for o in range(1, images):
        total = total + part_in[o].astype(F32) * clip[:, o : o + 1]
    sum_ref[...] = total
    pltpu.make_async_copy(norm_all, norm_all, norm_sem.at[0]).wait()


def local(draws, images, features, cotangent, time_index, mod_table, weight):
    pixels, in_width = features.shape[2:]
    out_width = cotangent.shape[3]
    table_rows = mod_table.shape[0]
    stratum = table_rows - (draws - 1) * table_rows // draws
    window = (stratum + 14) // 8
    piece = in_width // draws
    each = piece // images
    hops = draws // 4
    dma = pltpu.SemaphoreType.DMA
    return pl.pallas_call(
        functools.partial(kernel, draws, images, table_rows, window),
        out_shape=(
            pltpu.VMEM((each, out_width), F32),
            pltpu.VMEM(features.shape, BF16),
        ),
        in_specs=[pl.BlockSpec(memory_space=pltpu.HBM)] * 5,
        out_specs=(
            pl.BlockSpec(memory_space=pltpu.VMEM),
            pl.BlockSpec(memory_space=pltpu.VMEM),
        ),
        scratch_shapes=[
            pltpu.VMEM((pixels, in_width), BF16),
            pltpu.VMEM((pixels, out_width), BF16),
            pltpu.VMEM((1, 1), jnp.int32),
            pltpu.VMEM((window, 8, in_width), BF16),
            pltpu.VMEM((in_width, out_width), BF16),
            pltpu.VMEM((1, in_width), F32),
            pltpu.VMEM((pixels, out_width), BF16),
            pltpu.VMEM((in_width, out_width), F32),
            pltpu.VMEM((draws // 2, piece, out_width), BF16),
            pltpu.VMEM((draws // 2, piece, out_width), BF16),
            pltpu.VMEM((2, hops, piece, out_width), BF16),
            pltpu.VMEM((2, hops, piece, out_width), BF16),
            pltpu.VMEM((2, 2, hops, piece, out_width), BF16),
            pltpu.VMEM((2, 2, hops, piece, out_width), BF16),
            pltpu.VMEM((2, piece, out_width), F32),
            pltpu.VMEM((piece, out_width), BF16),
            pltpu.VMEM((piece, out_width), BF16),
            pltpu.VMEM((1, LANES), F32),
            pltpu.VMEM((images, 1, LANES), F32),
            pltpu.VMEM((1, LANES), F32),
            pltpu.VMEM((draws, 1, LANES), F32),
            pltpu.VMEM((images, each, out_width), BF16),
            pltpu.VMEM((images, each, out_width), BF16),
            dma((5,)),
            dma((draws // 2,)),
            dma((draws // 2,)),
            dma((2, hops)),
            dma((2, hops)),
            dma((2, 2, hops)),
            dma((2, 2, hops)),
            dma((2,)),
            dma((2,)),
            dma((2,)),
            dma((2,)),
        ],
        compiler_params=pltpu.CompilerParams(
            collective_id=0, has_side_effects=True, vmem_limit_bytes=60 * 2**20
        ),
        cost_estimate=pl.CostEstimate(
            flops=4 * pixels * in_width * out_width,
            bytes_accessed=2 * (2 * pixels * in_width + pixels * out_width + in_width * out_width),
            transcendentals=2 * pixels * in_width,
        ),
    )(
        features,
        cotangent,
        time_index,
        mod_table.reshape(table_rows // 8, 8, in_width),
        weight,
    )


def solution(mesh):
    in_specs = (
        P("img", "draw", None, None),
        P("img", "draw", None, None),
        P("img", "draw"),
        P(),
        P(),
    )
    out_specs = (P(("draw", "img"), None), P("img", "draw", None, None))
    body = functools.partial(local, mesh.shape["draw"], mesh.shape["img"])
    return jax.shard_map(body, mesh=mesh, in_specs=in_specs, out_specs=out_specs, check_vma=False)
```

```python
import functools
import math

import jax
import jax.numpy as jnp
from jax import lax
from jax.experimental import pallas as pl
from jax.experimental.pallas import tpu as pltpu
from jax.sharding import PartitionSpec as P

MESH = pl.DeviceIdType.MESH
F32 = jnp.float32
BF16 = jnp.bfloat16
LANES = 128
ROUNDS = 4
NEAR = {2: 1, 1: 0}
FAR = {8: 6, 7: 6, 6: 3, 5: 4, 4: 3, 3: 0}


def sigmoid(v):
    return 1.0 / (1.0 + jnp.exp(-v))


def tree_levels(tree):
    level = {}
    for node in sorted(tree, reverse=True):
        level[node] = max([level[c] + 1 for c in tree if tree[c] == node], default=0)
    for node in sorted(tree):
        if tree[node] in tree:
            level[node] = max(level[node], level[tree[node]] - 1)
    return level


def kernel(
    draws, images, table_rows, window,
    feat_hbm, cot_hbm, time_hbm, table_hbm, weight_hbm,
    sum_ref, gi_ref,
    feat, cot, when, rows, weight, gain, weighted, grad,
    first_out, first_in, xsend, xrecv, zsend, zrecv, root_in,
    share_out, share_in, norm_out, norm_in, part_out, part_in,
    load_sem, first_send, first_recv, xsend_sem, xrecv_sem, zsend_sem, zrecv_sem,
    root_recv, share_sem, norm_sem, part_sem, relay,
):
    in_width = feat.shape[1]
    out_width = cot.shape[1]
    ring = draws // 2
    half_rows = in_width // 2
    piece = in_width // draws
    each = piece // images
    k = lax.axis_index("draw")
    image = lax.axis_index("img")
    high = lax.div(k, ring)
    z = lax.rem(k, ring)

    def around(offset):
        return lax.rem(z + (offset + ring), ring)

    def at_z(offset):
        return {"draw": high * ring + around(offset)}

    partner = {"draw": (1 - high) * ring + z}

    first_row = lax.div(k * table_rows, draws)
    first_block = jnp.minimum(lax.div(first_row, 8), table_rows // 8 - window)
    loads = [
        pltpu.make_async_copy(time_hbm, when, load_sem.at[0]),
        pltpu.make_async_copy(table_hbm.at[pl.ds(first_block, window)], rows, load_sem.at[1]),
        pltpu.make_async_copy(cot_hbm.at[0, 0], cot, load_sem.at[2]),
        pltpu.make_async_copy(feat_hbm.at[0, 0], feat, load_sem.at[3]),
        pltpu.make_async_copy(weight_hbm, weight, load_sem.at[4]),
    ]
    for load in loads:
        load.start()

    apart = ring // 2
    turned = 1 - lax.div(around(ring // 4), apart)

    for way in range(2):
        xrecv[way, apart - 1] = jnp.zeros(xrecv.shape[2:], BF16)

    y, bits = lax.div(image, 4), lax.rem(image, 4)
    bit_x, bit_core = lax.div(bits, 2), lax.rem(bits, 2)
    planes = images // 4
    neighbours = [
        at_z(1),
        at_z(-1),
        {"img": lax.rem(y + 1, planes) * 4 + bits},
        {"img": lax.rem(y + planes - 1, planes) * 4 + bits},
        {"img": image + 2 - 4 * bit_x},
        {"img": image + 1 - 2 * bit_core},
    ]
    barrier = pltpu.get_barrier_semaphore()
    for device in [partner] + neighbours:
        pl.semaphore_signal(barrier, inc=1, device_id=device, device_id_type=MESH)

    def tell(turn):
        for device in neighbours:
            pl.semaphore_signal(relay.at[turn], inc=1, device_id=device, device_id_type=MESH)

    def hear(turn):
        pl.semaphore_wait(relay.at[turn], len(neighbours))

    for load in loads[:3]:
        load.wait()
    step = when[...]
    index = (
        lax.broadcasted_iota(jnp.int32, (window, 8, 1), 0) * 8
        + lax.broadcasted_iota(jnp.int32, (window, 8, 1), 1)
        + first_block * 8
    )
    chosen = jnp.where(index == step.reshape(1, 1, 1), rows[...].astype(F32), 0.0)
    gain[...] = 1.0 + jnp.sum(jnp.sum(chosen, axis=0), axis=0, keepdims=True)
    loss_scale = 1.0 + 2.0 * step.astype(F32) / (table_rows - 1)
    weighted[...] = (cot[...].astype(F32) * loss_scale).astype(BF16)
    loads[3].wait()

    def local_gradient(half):
        for n in range(half_rows // LANES):
            at = pl.ds(pl.multiple_of(half * half_rows + n * LANES, LANES), LANES)
            pre_act = feat[:, at].astype(F32) * gain[:, at]
            acts = (pre_act * sigmoid(pre_act)).astype(BF16)
            grad[at, :] = lax.dot_general(
                acts, weighted[...], (((0,), (0,)), ((), ())), preferred_element_type=F32
            )

    local_gradient(1 - high)
    pl.semaphore_wait(barrier, len(neighbours) + 1)
    tell(0)

    def own(half, offset):
        start = half * half_rows + around(offset) * piece
        return grad[pl.ds(pl.multiple_of(start, piece), piece), :]

    def first_copy(n):
        return pltpu.make_async_remote_copy(
            src_ref=first_out.at[n],
            dst_ref=first_in.at[n],
            send_sem=first_send.at[n],
            recv_sem=first_recv.at[n],
            device_id=partner,
            device_id_type=MESH,
        )

    def near_copy(half, way, node, hop):
        return pltpu.make_async_remote_copy(
            src_ref=zsend.at[half, way, node - 1],
            dst_ref=zrecv.at[half, way, node - 1],
            send_sem=zsend_sem.at[half, way, node - 1],
            recv_sem=zrecv_sem.at[half, way, node - 1],
            device_id=at_z(hop * (1 - 2 * way)),
            device_id_type=MESH,
        )

    def root_copy(half, way, hop, column):
        return pltpu.make_async_remote_copy(
            src_ref=zsend.at[half, way, hop - 1],
            dst_ref=root_in.at[column, way],
            send_sem=zsend_sem.at[half, way, hop - 1],
            recv_sem=root_recv.at[column, way],
            device_id={"draw": half * ring + around(hop * (1 - 2 * way))},
            device_id_type=MESH,
        )

    def far_copy(way, node, hop):
        part = pl.ds(0, piece)
        if node == apart:
            part = pl.ds(pl.multiple_of(way * (piece // 2), piece // 2), piece // 2)
        return pltpu.make_async_remote_copy(
            src_ref=xsend.at[way, node - 1, part],
            dst_ref=xrecv.at[way, node - 1, part],
            send_sem=xsend_sem.at[way, node - 1],
            recv_sem=xrecv_sem.at[way, node - 1],
            device_id=at_z(hop * (1 - 2 * way)),
            device_id_type=MESH,
        )

    def children(tree, node):
        return [c for c in tree if tree[c] == node]

    def near_sum(half, way, node, term):
        for child in children(NEAR, node):
            near_copy(half, way, child, child - node).wait_recv()
            term = term + zrecv[half, way, child - 1].astype(F32)
        return term

    def far_sum(way, node, term):
        for child in children(FAR, node):
            far_copy(way, child, child - node).wait_recv()
            term = term + xrecv[way, child - 1].astype(F32)
        return term

    def grad_input_block(block):
        at = pl.ds(block * LANES, LANES)
        back = lax.dot_general(
            weighted[...], weight[at, :], (((1,), (1,)), ((), ())), preferred_element_type=F32
        )
        scale = gain[:, at]
        pre_act = feat[:, at].astype(F32) * scale
        gate = sigmoid(pre_act)
        gi_ref[0, 0, :, at] = (back * gate * (1.0 + pre_act * (1.0 - gate)) * scale).astype(BF16)

    jobs = []
    for way in range(2):
        for node, level in tree_levels(NEAR).items():
            jobs += [(level, 0, -node, way, half) for half in range(2)]
        for node, level in tree_levels(FAR).items():
            jobs.append((level, 1, -node, way, 0))
    jobs.sort()
    sent = []
    known = 1
    offsets = [0]
    for _, kind, minus, way, _ in reversed(jobs):
        offset = (-minus if way == 0 else minus) % ring
        if kind == 1 and offset not in offsets:
            offsets.insert(0, offset)
    for offset in offsets:
        first_out[offset] = own(1 - high, offset).astype(BF16)
        sent.append(first_copy(offset))
        sent[-1].start()
    local_gradient(high)

    def greet_more(known):
        hear(known - 1)
        if known < ROUNDS:
            tell(known)
        return known + 1

    for at, (level, kind, minus, first, half) in enumerate(jobs):
        node = -minus
        hop = node - (FAR if kind else NEAR)[node]
        way = first + turned - 2 * first * turned
        offset = node * (1 - 2 * way)
        while known < (2 if kind == 0 and node == hop else hop):
            known = greet_more(known)
        if kind == 0:
            term = near_sum(half, way, node, own(half, offset))
            zsend[half, way, node - 1] = term.astype(BF16)
            if node == hop:
                copy = root_copy(half, way, hop, high)
            else:
                copy = near_copy(half, way, node, hop)
        else:
            slot = lax.rem(offset + ring, ring)
            if node < apart or first == 0:
                first_copy(slot).wait_recv()
            term = own(high, offset) + first_in[slot].astype(F32)
            xsend[way, node - 1] = far_sum(way, node, term).astype(BF16)
            copy = far_copy(way, node, hop)
        copy.start()
        sent.append(copy)
        if at + 1 == len(jobs) or jobs[at + 1][0] > level:
            if known < ROUNDS + 1:
                known = greet_more(known)

    while known < ROUNDS + 1:
        known = greet_more(known)

    mine = own(high, 0)
    first_copy(0).wait_recv()
    mine = mine + first_in[0].astype(F32)
    for way in range(2):
        (hop,) = children(NEAR, 0)
        for column in range(2):
            root_copy(0, way, hop, column).wait_recv()
            mine = mine + root_in[column, way].astype(F32)
    for way in range(2):
        mine = far_sum(way, 0, mine)
    mine = mine * (1.0 / draws)

    def finish():
        for copy in sent:
            copy.wait_send()


    square = mine * mine
    tile = square[:, 0:LANES]
    for c in range(1, out_width // LANES):
        tile = tile + square[:, c * LANES : (c + 1) * LANES]
    share_out[...] = jnp.sum(tile, axis=0, keepdims=True)

    def share_start(o, _):
        pltpu.make_async_remote_copy(
            src_ref=share_out,
            dst_ref=share_in.at[o],
            send_sem=share_sem.at[0],
            recv_sem=share_sem.at[1],
            device_id=at_z(o),
            device_id_type=MESH,
        ).start()
        return 0

    lax.fori_loop(1, ring, share_start, 0)
    for j in range(images):
        part_out[j] = mine[j * each : (j + 1) * each, :].astype(BF16)

    def part_start(o, _):
        to = lax.rem(image + o, images)
        pltpu.make_async_remote_copy(
            src_ref=part_out.at[to],
            dst_ref=part_in.at[o],
            send_sem=part_sem.at[0],
            recv_sem=part_sem.at[1],
            device_id={"img": to},
            device_id_type=MESH,
        ).start()
        return 0

    lax.fori_loop(1, images, part_start, 0)
    share_in[0] = share_out[...]
    part_in[0] = part_out[image]

    loads[4].wait()
    for block in range(in_width // LANES):
        grad_input_block(block)
    finish()
    part_all = part_in.at[pl.ds(1, images - 1)]
    pltpu.make_async_copy(part_all, part_all, part_sem.at[1]).wait()
    pltpu.make_async_copy(part_all, part_all, part_sem.at[0]).wait()
    share_all = share_in.at[pl.ds(1, ring - 1)]
    pltpu.make_async_copy(share_all, share_all, share_sem.at[1]).wait()

    norm_out[...] = jnp.sum(share_in[...], axis=0)

    def norm_copy(o, to):
        return pltpu.make_async_remote_copy(
            src_ref=norm_out,
            dst_ref=norm_in.at[o],
            send_sem=norm_sem.at[0],
            recv_sem=norm_sem.at[1],
            device_id=to,
            device_id_type=MESH,
        )

    def norm_start(o, _):
        to = lax.rem(image + o, images)
        norm_copy(images + o, {"draw": partner["draw"], "img": to}).start()
        norm_copy(o, {"img": to}).start()
        return 0

    lax.fori_loop(1, images, norm_start, 0)
    norm_copy(images, partner).start()
    norm_in[0] = norm_out[...]
    norm_all = norm_in.at[pl.ds(1, 2 * images - 1)]
    pltpu.make_async_copy(norm_all, norm_all, norm_sem.at[1]).wait()
    norm_sq = jnp.sum(norm_in[0:images] + norm_in[images:], axis=2, keepdims=True)
    bound = 0.3 * math.sqrt(in_width * out_width)
    clip = jnp.minimum(1.0, bound / jnp.sqrt(norm_sq + 1e-06))
    sum_ref[...] = jnp.sum(part_in[...].astype(F32) * clip, axis=0)
    pltpu.make_async_copy(share_all, share_all, share_sem.at[0]).wait()
    pltpu.make_async_copy(norm_all, norm_all, norm_sem.at[0]).wait()


def local(draws, images, features, cotangent, time_index, mod_table, weight):
    pixels, in_width = features.shape[2:]
    out_width = cotangent.shape[3]
    table_rows = mod_table.shape[0]
    stratum = table_rows - (draws - 1) * table_rows // draws
    window = (stratum + 14) // 8
    piece = in_width // draws
    each = piece // images
    hops = draws // 4
    dma = pltpu.SemaphoreType.DMA
    return pl.pallas_call(
        functools.partial(kernel, draws, images, table_rows, window),
        out_shape=(
            pltpu.VMEM((each, out_width), F32),
            pltpu.VMEM(features.shape, BF16),
        ),
        in_specs=[pl.BlockSpec(memory_space=pltpu.HBM)] * 5,
        out_specs=(
            pl.BlockSpec(memory_space=pltpu.VMEM),
            pl.BlockSpec(memory_space=pltpu.VMEM),
        ),
        scratch_shapes=[
            pltpu.VMEM((pixels, in_width), BF16),
            pltpu.VMEM((pixels, out_width), BF16),
            pltpu.VMEM((1, 1), jnp.int32),
            pltpu.VMEM((window, 8, in_width), BF16),
            pltpu.VMEM((in_width, out_width), BF16),
            pltpu.VMEM((1, in_width), F32),
            pltpu.VMEM((pixels, out_width), BF16),
            pltpu.VMEM((in_width, out_width), F32),
            pltpu.VMEM((draws // 2, piece, out_width), BF16),
            pltpu.VMEM((draws // 2, piece, out_width), BF16),
            pltpu.VMEM((2, hops, piece, out_width), BF16),
            pltpu.VMEM((2, hops, piece, out_width), BF16),
            pltpu.VMEM((2, 2, hops, piece, out_width), BF16),
            pltpu.VMEM((2, 2, hops, piece, out_width), BF16),
            pltpu.VMEM((2, 2, piece, out_width), BF16),
            pltpu.VMEM((1, LANES), F32),
            pltpu.VMEM((draws // 2, 1, LANES), F32),
            pltpu.VMEM((1, LANES), F32),
            pltpu.VMEM((2 * images, 1, LANES), F32),
            pltpu.VMEM((images, each, out_width), BF16),
            pltpu.VMEM((images, each, out_width), BF16),
            dma((5,)),
            dma((draws // 2,)),
            dma((draws // 2,)),
            dma((2, hops)),
            dma((2, hops)),
            dma((2, 2, hops)),
            dma((2, 2, hops)),
            dma((2, 2)),
            dma((2,)),
            dma((2,)),
            dma((2,)),
            pltpu.SemaphoreType.REGULAR((ROUNDS,)),
        ],
        compiler_params=pltpu.CompilerParams(
            collective_id=0, has_side_effects=True, vmem_limit_bytes=60 * 2**20
        ),
        cost_estimate=pl.CostEstimate(
            flops=4 * pixels * in_width * out_width,
            bytes_accessed=2 * (2 * pixels * in_width + pixels * out_width + in_width * out_width),
            transcendentals=2 * pixels * in_width,
        ),
    )(
        features,
        cotangent,
        time_index,
        mod_table.reshape(table_rows // 8, 8, in_width),
        weight,
    )


def solution(mesh):
    in_specs = (
        P("img", "draw", None, None),
        P("img", "draw", None, None),
        P("img", "draw"),
        P(),
        P(),
    )
    out_specs = (P(("draw", "img"), None), P("img", "draw", None, None))
    body = functools.partial(local, mesh.shape["draw"], mesh.shape["img"])
    return jax.shard_map(body, mesh=mesh, in_specs=in_specs, out_specs=out_specs, check_vma=False)
```

```python
import functools
import math

import jax
import jax.numpy as jnp
from jax import lax
from jax.experimental import pallas as pl
from jax.experimental.pallas import tpu as pltpu
from jax.sharding import PartitionSpec as P

MESH = pl.DeviceIdType.MESH
F32 = jnp.float32
BF16 = jnp.bfloat16
LANES = 128
ROUNDS = 4
NEAR = {2: 1, 1: 0}
FAR = {8: 6, 7: 6, 6: 3, 5: 4, 4: 3, 3: 0}


def sigmoid(v):
    return 1.0 / (1.0 + jnp.exp(-v))


def tree_levels(tree):
    level = {}
    for node in sorted(tree, reverse=True):
        level[node] = max([level[c] + 1 for c in tree if tree[c] == node], default=0)
    for node in sorted(tree):
        if tree[node] in tree:
            level[node] = max(level[node], level[tree[node]] - 1)
    return level


def kernel(
    draws, images, table_rows, window,
    feat_hbm, cot_hbm, time_hbm, table_hbm, weight_hbm,
    sum_ref, gi_ref,
    feat, cot, when, rows, weight, gain, weighted, grad,
    first_out, first_in, xsend, xrecv, zsend, zrecv, root_in,
    share_out, share_in, norm_out, norm_in, part_out, part_in,
    load_sem, first_send, first_recv, xsend_sem, xrecv_sem, zsend_sem, zrecv_sem,
    root_recv, share_sem, norm_sem, part_sem, relay,
):
    in_width = feat.shape[1]
    out_width = cot.shape[1]
    ring = draws // 2
    half_rows = in_width // 2
    piece = in_width // draws
    each = piece // images
    k = lax.axis_index("draw")
    image = lax.axis_index("img")
    high = lax.div(k, ring)
    z = lax.rem(k, ring)

    def around(offset):
        return lax.rem(z + (offset + ring), ring)

    def at_z(offset):
        return {"draw": high * ring + around(offset)}

    partner = {"draw": (1 - high) * ring + z}

    first_row = lax.div(k * table_rows, draws)
    first_block = jnp.minimum(lax.div(first_row, 8), table_rows // 8 - window)
    loads = [
        pltpu.make_async_copy(time_hbm, when, load_sem.at[0]),
        pltpu.make_async_copy(table_hbm.at[pl.ds(first_block, window)], rows, load_sem.at[1]),
        pltpu.make_async_copy(cot_hbm.at[0, 0], cot, load_sem.at[2]),
        pltpu.make_async_copy(feat_hbm.at[0, 0], feat, load_sem.at[3]),
        pltpu.make_async_copy(weight_hbm, weight, load_sem.at[4]),
    ]
    for load in loads[:4]:
        load.start()

    apart = ring // 2
    turned = 1 - lax.div(around(ring // 4), apart)

    for way in range(2):
        xrecv[way, apart - 1] = jnp.zeros(xrecv.shape[2:], BF16)

    y, bits = lax.div(image, 4), lax.rem(image, 4)
    bit_x, bit_core = lax.div(bits, 2), lax.rem(bits, 2)
    planes = images // 4
    neighbours = [
        at_z(1),
        at_z(-1),
        {"img": lax.rem(y + 1, planes) * 4 + bits},
        {"img": lax.rem(y + planes - 1, planes) * 4 + bits},
        {"img": image + 2 - 4 * bit_x},
        {"img": image + 1 - 2 * bit_core},
    ]
    barrier = pltpu.get_barrier_semaphore()
    for device in [partner] + neighbours:
        pl.semaphore_signal(barrier, inc=1, device_id=device, device_id_type=MESH)

    def tell(turn):
        for device in neighbours:
            pl.semaphore_signal(relay.at[turn], inc=1, device_id=device, device_id_type=MESH)

    def hear(turn):
        pl.semaphore_wait(relay.at[turn], len(neighbours))

    for load in loads[:3]:
        load.wait()
    step = when[...]
    index = (
        lax.broadcasted_iota(jnp.int32, (window, 8, 1), 0) * 8
        + lax.broadcasted_iota(jnp.int32, (window, 8, 1), 1)
        + first_block * 8
    )
    chosen = jnp.where(index == step.reshape(1, 1, 1), rows[...].astype(F32), 0.0)
    gain[...] = 1.0 + jnp.sum(jnp.sum(chosen, axis=0), axis=0, keepdims=True)
    loss_scale = 1.0 + 2.0 * step.astype(F32) / (table_rows - 1)
    weighted[...] = (cot[...].astype(F32) * loss_scale).astype(BF16)
    loads[3].wait()

    def local_gradient(half):
        for n in range(half_rows // LANES):
            at = pl.ds(pl.multiple_of(half * half_rows + n * LANES, LANES), LANES)
            pre_act = feat[:, at].astype(F32) * gain[:, at]
            acts = (pre_act * sigmoid(pre_act)).astype(BF16)
            grad[at, :] = lax.dot_general(
                acts, weighted[...], (((0,), (0,)), ((), ())), preferred_element_type=F32
            )

    local_gradient(1 - high)
    pl.semaphore_wait(barrier, len(neighbours) + 1)
    tell(0)

    def own(half, offset):
        start = half * half_rows + around(offset) * piece
        return grad[pl.ds(pl.multiple_of(start, piece), piece), :]

    def first_copy(n):
        return pltpu.make_async_remote_copy(
            src_ref=first_out.at[n],
            dst_ref=first_in.at[n],
            send_sem=first_send.at[n],
            recv_sem=first_recv.at[n],
            device_id=partner,
            device_id_type=MESH,
        )

    def near_copy(half, way, node, hop):
        return pltpu.make_async_remote_copy(
            src_ref=zsend.at[half, way, node - 1],
            dst_ref=zrecv.at[half, way, node - 1],
            send_sem=zsend_sem.at[half, way, node - 1],
            recv_sem=zrecv_sem.at[half, way, node - 1],
            device_id=at_z(hop * (1 - 2 * way)),
            device_id_type=MESH,
        )

    def root_copy(half, way, hop, column):
        return pltpu.make_async_remote_copy(
            src_ref=zsend.at[half, way, hop - 1],
            dst_ref=root_in.at[column, way],
            send_sem=zsend_sem.at[half, way, hop - 1],
            recv_sem=root_recv.at[column, way],
            device_id={"draw": half * ring + around(hop * (1 - 2 * way))},
            device_id_type=MESH,
        )

    def far_copy(way, node, hop):
        part = pl.ds(0, piece)
        if node == apart:
            part = pl.ds(pl.multiple_of(way * (piece // 2), piece // 2), piece // 2)
        return pltpu.make_async_remote_copy(
            src_ref=xsend.at[way, node - 1, part],
            dst_ref=xrecv.at[way, node - 1, part],
            send_sem=xsend_sem.at[way, node - 1],
            recv_sem=xrecv_sem.at[way, node - 1],
            device_id=at_z(hop * (1 - 2 * way)),
            device_id_type=MESH,
        )

    def children(tree, node):
        return [c for c in tree if tree[c] == node]

    def near_sum(half, way, node, term):
        for child in children(NEAR, node):
            near_copy(half, way, child, child - node).wait_recv()
            term = term + zrecv[half, way, child - 1].astype(F32)
        return term

    def far_sum(way, node, term):
        for child in children(FAR, node):
            far_copy(way, child, child - node).wait_recv()
            term = term + xrecv[way, child - 1].astype(F32)
        return term

    def grad_input_block(block):
        at = pl.ds(block * LANES, LANES)
        back = lax.dot_general(
            weighted[...], weight[at, :], (((1,), (1,)), ((), ())), preferred_element_type=F32
        )
        scale = gain[:, at]
        pre_act = feat[:, at].astype(F32) * scale
        gate = sigmoid(pre_act)
        gi_ref[0, 0, :, at] = (back * gate * (1.0 + pre_act * (1.0 - gate)) * scale).astype(BF16)

    jobs = []
    for way in range(2):
        for node, level in tree_levels(NEAR).items():
            jobs += [(level, 0, -node, way, half) for half in range(2)]
        for node, level in tree_levels(FAR).items():
            jobs.append((level, 1, -node, way, 0))
    jobs.sort()
    sent = []
    known = 1
    offsets = [0]
    for _, kind, minus, way, _ in reversed(jobs):
        offset = (-minus if way == 0 else minus) % ring
        if kind == 1 and offset not in offsets:
            offsets.insert(0, offset)
    for offset in offsets:
        first_out[offset] = own(1 - high, offset).astype(BF16)
        sent.append(first_copy(offset))
        sent[-1].start()
    local_gradient(high)
    loads[4].start()

    def greet_more(known):
        hear(known - 1)
        if known < ROUNDS:
            tell(known)
        return known + 1

    for at, (level, kind, minus, first, half) in enumerate(jobs):
        node = -minus
        hop = node - (FAR if kind else NEAR)[node]
        way = first + turned - 2 * first * turned
        offset = node * (1 - 2 * way)
        while known < (2 if kind == 0 and node == hop else hop):
            known = greet_more(known)
        if kind == 0:
            term = near_sum(half, way, node, own(half, offset))
            zsend[half, way, node - 1] = term.astype(BF16)
            if node == hop:
                copy = root_copy(half, way, hop, high)
            else:
                copy = near_copy(half, way, node, hop)
        else:
            slot = lax.rem(offset + ring, ring)
            if node < apart or first == 0:
                first_copy(slot).wait_recv()
            term = own(high, offset) + first_in[slot].astype(F32)
            xsend[way, node - 1] = far_sum(way, node, term).astype(BF16)
            copy = far_copy(way, node, hop)
        copy.start()
        sent.append(copy)

    while known < ROUNDS + 1:
        known = greet_more(known)

    mine = own(high, 0)
    first_copy(0).wait_recv()
    mine = mine + first_in[0].astype(F32)
    for way in range(2):
        (hop,) = children(NEAR, 0)
        for column in range(2):
            root_copy(0, way, hop, column).wait_recv()
            mine = mine + root_in[column, way].astype(F32)
    for way in range(2):
        mine = far_sum(way, 0, mine)
    mine = mine * (1.0 / draws)

    def finish():
        for copy in sent:
            copy.wait_send()


    square = mine * mine
    tile = square[:, 0:LANES]
    for c in range(1, out_width // LANES):
        tile = tile + square[:, c * LANES : (c + 1) * LANES]
    share_out[...] = jnp.sum(tile, axis=0, keepdims=True)

    def share_start(o, _):
        pltpu.make_async_remote_copy(
            src_ref=share_out,
            dst_ref=share_in.at[o],
            send_sem=share_sem.at[0],
            recv_sem=share_sem.at[1],
            device_id=at_z(o),
            device_id_type=MESH,
        ).start()
        return 0

    lax.fori_loop(1, ring, share_start, 0)
    for j in range(images):
        part_out[j] = mine[j * each : (j + 1) * each, :].astype(BF16)

    def part_start(o, _):
        to = lax.rem(image + o, images)
        pltpu.make_async_remote_copy(
            src_ref=part_out.at[to],
            dst_ref=part_in.at[o],
            send_sem=part_sem.at[0],
            recv_sem=part_sem.at[1],
            device_id={"img": to},
            device_id_type=MESH,
        ).start()
        return 0

    lax.fori_loop(1, images, part_start, 0)
    share_in[0] = share_out[...]
    part_in[0] = part_out[image]

    loads[4].wait()
    for block in range(in_width // LANES):
        grad_input_block(block)
    finish()
    part_all = part_in.at[pl.ds(1, images - 1)]
    pltpu.make_async_copy(part_all, part_all, part_sem.at[1]).wait()
    pltpu.make_async_copy(part_all, part_all, part_sem.at[0]).wait()
    share_all = share_in.at[pl.ds(1, ring - 1)]
    pltpu.make_async_copy(share_all, share_all, share_sem.at[1]).wait()

    norm_out[...] = jnp.sum(share_in[...], axis=0)

    def norm_copy(o, to):
        return pltpu.make_async_remote_copy(
            src_ref=norm_out,
            dst_ref=norm_in.at[o],
            send_sem=norm_sem.at[0],
            recv_sem=norm_sem.at[1],
            device_id=to,
            device_id_type=MESH,
        )

    def norm_start(o, _):
        to = lax.rem(image + o, images)
        norm_copy(images + o, {"draw": partner["draw"], "img": to}).start()
        norm_copy(o, {"img": to}).start()
        return 0

    lax.fori_loop(1, images, norm_start, 0)
    norm_copy(images, partner).start()
    norm_in[0] = norm_out[...]
    norm_all = norm_in.at[pl.ds(1, 2 * images - 1)]
    pltpu.make_async_copy(norm_all, norm_all, norm_sem.at[1]).wait()
    norm_sq = jnp.sum(norm_in[0:images] + norm_in[images:], axis=2, keepdims=True)
    bound = 0.3 * math.sqrt(in_width * out_width)
    clip = jnp.minimum(1.0, bound / jnp.sqrt(norm_sq + 1e-06))
    sum_ref[...] = jnp.sum(part_in[...].astype(F32) * clip, axis=0)
    pltpu.make_async_copy(share_all, share_all, share_sem.at[0]).wait()
    pltpu.make_async_copy(norm_all, norm_all, norm_sem.at[0]).wait()


def local(draws, images, features, cotangent, time_index, mod_table, weight):
    pixels, in_width = features.shape[2:]
    out_width = cotangent.shape[3]
    table_rows = mod_table.shape[0]
    stratum = table_rows - (draws - 1) * table_rows // draws
    window = (stratum + 14) // 8
    piece = in_width // draws
    each = piece // images
    hops = draws // 4
    dma = pltpu.SemaphoreType.DMA
    return pl.pallas_call(
        functools.partial(kernel, draws, images, table_rows, window),
        out_shape=(
            pltpu.VMEM((each, out_width), F32),
            pltpu.VMEM(features.shape, BF16),
        ),
        in_specs=[pl.BlockSpec(memory_space=pltpu.HBM)] * 5,
        out_specs=(
            pl.BlockSpec(memory_space=pltpu.VMEM),
            pl.BlockSpec(memory_space=pltpu.VMEM),
        ),
        scratch_shapes=[
            pltpu.VMEM((pixels, in_width), BF16),
            pltpu.VMEM((pixels, out_width), BF16),
            pltpu.VMEM((1, 1), jnp.int32),
            pltpu.VMEM((window, 8, in_width), BF16),
            pltpu.VMEM((in_width, out_width), BF16),
            pltpu.VMEM((1, in_width), F32),
            pltpu.VMEM((pixels, out_width), BF16),
            pltpu.VMEM((in_width, out_width), F32),
            pltpu.VMEM((draws // 2, piece, out_width), BF16),
            pltpu.VMEM((draws // 2, piece, out_width), BF16),
            pltpu.VMEM((2, hops, piece, out_width), BF16),
            pltpu.VMEM((2, hops, piece, out_width), BF16),
            pltpu.VMEM((2, 2, hops, piece, out_width), BF16),
            pltpu.VMEM((2, 2, hops, piece, out_width), BF16),
            pltpu.VMEM((2, 2, piece, out_width), BF16),
            pltpu.VMEM((1, LANES), F32),
            pltpu.VMEM((draws // 2, 1, LANES), F32),
            pltpu.VMEM((1, LANES), F32),
            pltpu.VMEM((2 * images, 1, LANES), F32),
            pltpu.VMEM((images, each, out_width), BF16),
            pltpu.VMEM((images, each, out_width), BF16),
            dma((5,)),
            dma((draws // 2,)),
            dma((draws // 2,)),
            dma((2, hops)),
            dma((2, hops)),
            dma((2, 2, hops)),
            dma((2, 2, hops)),
            dma((2, 2)),
            dma((2,)),
            dma((2,)),
            dma((2,)),
            pltpu.SemaphoreType.REGULAR((ROUNDS,)),
        ],
        compiler_params=pltpu.CompilerParams(
            collective_id=0, has_side_effects=True, vmem_limit_bytes=60 * 2**20
        ),
        cost_estimate=pl.CostEstimate(
            flops=4 * pixels * in_width * out_width,
            bytes_accessed=2 * (2 * pixels * in_width + pixels * out_width + in_width * out_width),
            transcendentals=2 * pixels * in_width,
        ),
    )(
        features,
        cotangent,
        time_index,
        mod_table.reshape(table_rows // 8, 8, in_width),
        weight,
    )


def solution(mesh):
    in_specs = (
        P("img", "draw", None, None),
        P("img", "draw", None, None),
        P("img", "draw"),
        P(),
        P(),
    )
    out_specs = (P(("draw", "img"), None), P("img", "draw", None, None))
    body = functools.partial(local, mesh.shape["draw"], mesh.shape["img"])
    return jax.shard_map(body, mesh=mesh, in_specs=in_specs, out_specs=out_specs, check_vma=False)
```
